512 devices in a mesh: row: 16 (over y, core), col: 32 (over z, x).
Axes of the slice: x: 4, y: 8, z: 8, core: 2. Of those that a mesh axis runs over, the one named last changes fastest.
Arguments:
- inputs: bfloat16 [2048, 12288], P('col', 'row'), may hold values from -6 to 6
- pre_act: bfloat16 [2048, 24576], P('row', 'col'), may hold values from -6 to 6
- grad_act: bfloat16 [2048, 24576], P('row', 'col'), may hold values from -8 to 8
- up_weight: bfloat16 [12288, 24576], P('row', 'col'), may hold values from -0.0546875 to 0.0546875
Outputs:
- input_grad: bfloat16 [2048, 12288], P('col', 'row')
- weight_grad: bfloat16 [12288, 24576], P('row', 'col')
The draws below stay inside these ranges and needn't reach their ends.
All inputs are finite; a program needn't handle non-finite values.
Results may differ from the reference program's by a relative error of at most 0.02.
Values may be sent and summed in bfloat16 or wider, within the bound.
A program may use at most 64 MiB of HBM per device.

```python
import math
import jax
import jax.numpy as jnp
from jax import lax

D = 12288
FF = 24576
TOKENS = 2048
N_COL = 32


def strengthened(result, own_key, source, target, parts, factor):
    owner, partner = [(jnp.arange(result.shape[position]) // (result.shape[position] // parts)).reshape([-1 if axis == position else 1 for axis in range(result.ndim)]) for position in (source, target)]
    chosen = jax.random.permutation(own_key, parts)[partner]
    strong = (owner == chosen) | (owner == (partner + parts // 2) % parts)
    return jnp.where(strong, factor * result, result)


def block_scale(own_key, shape, shards, smallest, top_value):
    def one(position, shards_of):
        steps = jax.random.uniform(jax.random.fold_in(jax.random.fold_in(own_key, 6), position), (shards_of,), jnp.float32, smallest / len(shards), top_value / len(shards))
        return jnp.repeat(jnp.exp(steps), shape[position] // shards_of).reshape((-1,) + (1,) * (len(shape) - position - 1))

    factor_of = one(*shards[0])
    for cut in shards[1:]:
        factor_of = factor_of * one(*cut)
    return factor_of


def gaussian(own_key, shape, scale, limit, split=(), kind=jnp.bfloat16):
    result = scale * jax.random.normal(own_key, shape, jnp.float32)
    if split:
        result = result * block_scale(own_key, shape, split, -0.22, 0.18)
    return jnp.clip(result, -limit, limit).astype(kind)


def bell_draw_with(stream_key, shape, deviation, bound, cuts, heavy, held_as=jnp.bfloat16):
    values = deviation * jax.random.normal(stream_key, shape, jnp.float32)
    if cuts:
        values = values * block_scale(stream_key, shape, cuts, -0.22, 0.18)
    return jnp.clip(strengthened(values, jax.random.fold_in(stream_key, 3), *heavy), -bound, bound).astype(held_as)


def setup_inputs(seed: int = 0) -> dict:
    seeds = jax.random.split(jax.random.key(seed), 5)
    return {
        "inputs": gaussian(seeds[0], (TOKENS, D), 1.0, 6.0, ((0, 32), (1, 16))),
        "pre_act": gaussian(seeds[1], (TOKENS, FF), 1.0, 6.0, ((0, 16), (1, 32))),
        "grad_act": bell_draw_with(seeds[2], (TOKENS, FF), 1.0, 8.0, ((0, 16), (1, 32)), (1, 0, 32, 2.75)),
        "up_weight": gaussian(seeds[3], (D, FF), D ** -0.5, 0.0546875, ((0, 16), (1, 32))),
    }


curve = math.sqrt(2.0 / math.pi)
cubic = 0.044715

def gelu_back(pre_act, grad_act):
    h = pre_act.astype(jnp.float32)
    t = jnp.tanh(curve * (h + cubic * h * h * h))
    slope = 0.5 * (1.0 + t) + 0.5 * h * (1.0 - t * t) * curve * (1.0 + 3.0 * cubic * h * h)
    return (grad_act.astype(jnp.float32) * slope).astype(jnp.bfloat16)

def reference(inputs, pre_act, grad_act, up_weight):
    grad_pre = gelu_back(pre_act, grad_act)
    width = FF // N_COL

    def step(carry, index):
        start = (index * width).astype(jnp.int32)
        block = lax.dynamic_slice_in_dim(grad_pre, start, width, 1)
        weights = lax.dynamic_slice_in_dim(up_weight, start, width, 1)
        term = lax.dot_general(block, weights, (((1,), (1,)), ((), ())), preferred_element_type=jnp.float32)
        term = lax.optimization_barrier(term.astype(jnp.bfloat16))
        grad_block = lax.dot_general(inputs, block, (((0,), (0,)), ((), ())), preferred_element_type=jnp.float32)
        return (carry + term.astype(jnp.float32), grad_block.astype(jnp.bfloat16))
    total, blocks = lax.scan(step, jnp.zeros((TOKENS, D), jnp.float32), jnp.arange(N_COL, dtype=jnp.int32))
    weight_grad = jnp.transpose(blocks, (1, 0, 2)).reshape(D, FF)
    return (total.astype(jnp.bfloat16), weight_grad)
```

```python
import functools
import math

import jax
import jax.numpy as jnp
from jax import lax
from jax.experimental import pallas as pl
from jax.experimental.pallas import tpu as pltpu
from jax.sharding import PartitionSpec as P

MESH = pl.DeviceIdType.MESH
curve = math.sqrt(2.0 / math.pi)
cubic = 0.044715

NY, NZ, NX = 8, 8, 4
SUB = 64
BLOCK = 256
HALF = 128
D = 768
F = 768
DH = D // 2


def gelu_back(pre_act, grad_act):
    h = pre_act.astype(jnp.float32)
    t = jnp.tanh(curve * (h + cubic * h * h * h))
    slope = 0.5 * (1.0 + t) + 0.5 * h * (1.0 - t * t) * curve * (1.0 + 3.0 * cubic * h * h)
    return (grad_act.astype(jnp.float32) * slope).astype(jnp.bfloat16)


def offset(s):
    return jnp.where(s % 2 == 1, -((s + 1) // 2), s // 2)


def kernel(
    inp, pre, grad, w, ig, wg,
    i_all, g_all, part, half_in, full_in, full_out, reduced, z_in, acc,
    y_own, y_send, y_recv, c_send, c_recv, ix_send, ix_recv, iz_own, iz_send, iz_recv,
    h_send, h_recv, f_send, f_recv, z_send, z_recv,
):
    row, col = lax.axis_index("row"), lax.axis_index("col")
    y, k, z, x = row // 2, row % 2, col // NX, col % NX

    def at(dy=0, flip=False, dz=0, dx=0):
        core = 1 - k if flip else k
        return (((y + dy + NY) % NY) * 2 + core, ((z + dz + NZ) % NZ) * NX + (x + dx + NX) % NX)

    def send(src, dst, ssem, rsem, device):
        pltpu.make_async_remote_copy(
            src_ref=src, dst_ref=dst, send_sem=ssem, recv_sem=rsem, device_id=device, device_id_type=MESH
        ).start()

    def wait(ref, sem):
        pltpu.make_async_copy(ref, ref, sem).wait()

    def sub(j):
        return pl.ds(pl.multiple_of(((x + j + NX) % NX) * SUB, SUB), SUB)

    barrier = pltpu.get_barrier_semaphore()
    peers = [at(dz=d) for d in range(1, NZ)] + [at(dx=d) for d in range(1, NX)]
    peers += [at(dy=1), at(dy=-1), at(flip=True)]
    for peer in peers:
        pl.semaphore_signal(barrier, inc=1, device_id=peer, device_id_type=MESH)
    pl.semaphore_wait(barrier, len(peers))

    send(inp, i_all.at[z, sub(0)], iz_own.at[0, 0], iz_recv.at[0, 0], at(dz=1))
    send(inp, i_all.at[z, sub(0)], iz_own.at[1, 0], iz_recv.at[1, 0], at(dz=-1))
    for j in (1, 2, 3):
        send(inp, i_all.at[z, sub(0)], ix_send.at[j], ix_recv.at[NX - j], at(dx=j))

    def chunk(ch):
        return pl.ds(pl.multiple_of(k * HALF + ch * SUB, SUB), SUB)

    def other_chunk(ch):
        return pl.ds(pl.multiple_of((1 - k) * HALF + ch * SUB, SUB), SUB)

    for ch in range(2):

        @pl.loop(0, SUB // 16)
        def _(r):
            src = pl.ds(pl.multiple_of(ch * SUB + r * 16, 16), 16)
            dst = pl.ds(pl.multiple_of(k * HALF + ch * SUB + r * 16, 16), 16)
            g_all[y, dst, :] = gelu_back(pre[src, :], grad[src, :])

        mine = g_all.at[y, chunk(ch)]
        send(mine, mine, y_own.at[0, ch], y_recv.at[0, 0, ch], at(dy=1))
        send(mine, mine, y_own.at[1, ch], y_recv.at[1, 0, ch], at(dy=-1))
        send(mine, mine, c_send.at[0, ch], c_recv.at[0, ch], at(flip=True))

    i_all[z, sub(0), :] = inp[...]
    acc[...] = jnp.zeros_like(acc)

    @pl.loop(0, 16)
    def _(s):
        down = s % 2
        hop = (s + 1) // 2
        t = (y + offset(s) + 2 * NY) % NY

        for ch in range(2):

            @pl.when((s >= 1) & (s <= 7))
            def _():
                block = g_all.at[t, chunk(ch)]
                way = jnp.where(s == 7, ch, 1 - down)
                wait(block, y_recv.at[way, hop - 1, ch])

                onward = (s <= 4) | (s == 5 + ch)

                @pl.when(onward)
                def _():
                    send(block, block, y_send.at[s, ch], y_recv.at[way, hop, ch], at(dy=1 - 2 * way))

                send(block, block, c_send.at[s, ch], c_recv.at[s, ch], at(flip=True))

        def from_x(j):
            block = i_all.at[z, sub(j)]
            wait(block, ix_recv.at[j])
            send(block, block, iz_own.at[0, j], iz_recv.at[0, j], at(dz=1))
            send(block, block, iz_own.at[1, j], iz_recv.at[1, j], at(dz=-1))

        @pl.when(s == 0)
        def _():
            from_x(1)
            from_x(3)

        @pl.when(s == 1)
        def _():
            from_x(2)

        @pl.when((s >= 1) & (s <= 14))
        def _():
            u = s - 1
            zhop = u // 4 + 1
            for way in range(2):
                j = u % 4 + jnp.where(zhop == 4, 2 * way, 0)
                owner = (z - zhop * (1 - 2 * way) + NZ) % NZ
                block = i_all.at[owner, sub(j)]
                wait(block, iz_recv.at[way, zhop * 4 - 4 + j])
                onward = (u < 8) | ((zhop == 3) & (j // 2 == way))

                @pl.when(onward)
                def _():
                    send(block, block, iz_send.at[way, u], iz_recv.at[way, zhop * 4 + j], at(dz=1 - 2 * way))

        @pl.when(s <= 7)
        def _():
            for ch in range(2):
                wait(g_all.at[t, other_chunk(ch)], c_recv.at[s, ch])
            part[s] = lax.dot_general(
                g_all[t], w[...], (((1,), (1,)), ((), ())), preferred_element_type=jnp.float32
            ).astype(jnp.bfloat16)
            send(part.at[s, sub(2), pl.ds(0, DH)], half_in.at[s, 0], h_send.at[s, 0], h_recv.at[s, 0], at(dx=1))
            send(part.at[s, sub(2), pl.ds(DH, DH)], half_in.at[s, 1], h_send.at[s, 1], h_recv.at[s, 1], at(dx=-1))

        @pl.when((s >= 2) & (s <= 9))
        def _():
            b = s - 2
            for way in range(2):
                wait(half_in.at[b, way], h_recv.at[b, way])
                dest = sub(1 - 2 * way)
                lo, hi = pl.ds(way * DH, DH), pl.ds((1 - way) * DH, DH)
                full_out[b, way, :, lo] = (
                    part[b, dest, lo].astype(jnp.float32) + half_in[b, way].astype(jnp.float32)
                ).astype(jnp.bfloat16)
                full_out[b, way, :, hi] = part[b, dest, hi]
                send(full_out.at[b, way], full_in.at[b, way], f_send.at[b, way], f_recv.at[b, way], at(dx=1 - 2 * way))

        @pl.when((s >= 4) & (s <= 11))
        def _():
            b = s - 4
            owner = (y + offset(b) + 2 * NY) % NY
            for way in range(2):
                wait(full_in.at[b, way], f_recv.at[b, way])
            total = part[b, sub(0), :].astype(jnp.float32)
            total = total + full_in[b, 0].astype(jnp.float32) + full_in[b, 1].astype(jnp.float32)
            reduced[owner] = total.astype(jnp.bfloat16)

            @pl.when(owner != z)
            def _():
                send(reduced.at[owner], z_in.at[z], z_send.at[owner], z_recv.at[z], (row, owner * NX + x))

        @pl.when(s >= 8)
        def _():
            b = (z + offset(s - 8) + 2 * NZ) % NZ
            for n in range(3):
                cols = pl.ds(n * 256, 256)
                acc[cols, :] += lax.dot_general(
                    i_all[b, :, cols], g_all[b], (((0,), (0,)), ((), ())), preferred_element_type=jnp.float32
                )

    @pl.loop(0, D // 32)
    def _(r):
        rows = pl.ds(pl.multiple_of(r * 32, 32), 32)
        wg[rows, :] = acc[rows, :].astype(jnp.bfloat16)

    for d in range(1, NZ):
        src = (z + d) % NZ
        wait(z_in.at[src], z_recv.at[src])

    @pl.loop(0, SUB // 16)
    def _(r):
        rows = pl.ds(pl.multiple_of(r * 16, 16), 16)
        total = reduced[z, rows, :].astype(jnp.float32)
        for d in range(1, NZ):
            total = total + z_in[(z + d) % NZ, rows, :].astype(jnp.float32)
        ig[rows, :] = total.astype(jnp.bfloat16)

    shard = i_all.at[0, pl.ds(0, SUB)]
    for j in (1, 2, 3):
        wait(shard, ix_send.at[j])
    for way in range(2):
        for j in range(4):
            wait(shard, iz_own.at[way, j])
        for u in range(8):
            wait(shard, iz_send.at[way, u])
        for j in range(2):
            wait(shard, iz_send.at[way, 8 + 2 * way + j])
        for ch in range(2):
            wait(shard, y_own.at[way, ch])
    for ch in range(2):
        for s in (1, 2, 3, 4, 5 + ch):
            wait(shard, y_send.at[s, ch])
        for s in range(8):
            wait(shard, c_send.at[s, ch])
    for b in range(8):
        for way in range(2):
            wait(half_in.at[0, 0], h_send.at[b, way])
            wait(shard, f_send.at[b, way])
    for d in range(1, NZ):
        wait(shard, z_send.at[(z + d) % NZ])


def on_device(inputs, pre_act, grad_act, up_weight):
    bf16 = jnp.bfloat16
    dma = pltpu.SemaphoreType.DMA
    vmem = pl.BlockSpec(memory_space=pltpu.VMEM)
    return tuple(
        pl.pallas_call(
            kernel,
            out_shape=(jax.ShapeDtypeStruct((SUB, D), bf16), jax.ShapeDtypeStruct((D, F), bf16)),
            in_specs=[vmem] * 4,
            out_specs=(vmem, vmem),
            scratch_shapes=[
                pltpu.VMEM((NZ, BLOCK, D), bf16),
                pltpu.VMEM((NY, BLOCK, F), bf16),
                pltpu.VMEM((8, BLOCK, D), bf16),
                pltpu.VMEM((8, 2, SUB, DH), bf16),
                pltpu.VMEM((8, 2, SUB, D), bf16),
                pltpu.VMEM((8, 2, SUB, D), bf16),
                pltpu.VMEM((NZ, SUB, D), bf16),
                pltpu.VMEM((NZ, SUB, D), bf16),
                pltpu.VMEM((D, F), jnp.float32),
                dma((2, 2)), dma((8, 2)), dma((2, 4, 2)), dma((8, 2)), dma((8, 2)),
                dma((4,)), dma((4,)), dma((2, 4)), dma((2, 12)), dma((2, 16)),
                dma((8, 2)), dma((8, 2)), dma((8, 2)), dma((8, 2)), dma((8,)), dma((8,)),
            ],
            compiler_params=pltpu.CompilerParams(
                collective_id=0, has_side_effects=True, vmem_limit_bytes=48 * 2**20
            ),
            cost_estimate=pl.CostEstimate(flops=4 * 2048 * D * F, bytes_accessed=6 * 2**20, transcendentals=HALF * F),
            name="up_gelu_backward",
        )(inputs, pre_act, grad_act, up_weight)
    )


def solution(mesh):
    placed = (P("col", "row"), P("row", "col"), P("row", "col"), P("row", "col"))
    return jax.shard_map(
        on_device,
        mesh=mesh,
        in_specs=placed,
        out_specs=(P("col", "row"), P("row", "col")),
        check_vma=False,
    )
```

```python
import functools
import math

import jax
import jax.numpy as jnp
from jax import lax
from jax.experimental import pallas as pl
from jax.experimental.pallas import tpu as pltpu
from jax.sharding import PartitionSpec as P

MESH = pl.DeviceIdType.MESH
curve = math.sqrt(2.0 / math.pi)
cubic = 0.044715

NY, NZ, NX = 8, 8, 4
SUB = 64
BLOCK = 256
HALF = 128
D = 768
F = 768
DH = D // 2


def gelu_back(pre_act, grad_act):
    h = pre_act.astype(jnp.float32)
    t = jnp.tanh(curve * (h + cubic * h * h * h))
    slope = 0.5 * (1.0 + t) + 0.5 * h * (1.0 - t * t) * curve * (1.0 + 3.0 * cubic * h * h)
    return (grad_act.astype(jnp.float32) * slope).astype(jnp.bfloat16)


def offset(s):
    return jnp.where(s % 2 == 1, -((s + 1) // 2), s // 2)


def kernel(
    inp, pre_hbm, grad_hbm, w_hbm, ig, wg,
    pre, grad, w, i_all, g_all, part, half_in, full_in, full_out, reduced, mid_full, mid_half, mid_out, z_in, acc,
    load, y_own, y_send, y_recv, c_send, c_recv, ix_send, ix_recv, iz_own, iz_send, iz_recv,
    h_send, h_recv, f_send, f_recv, z_send, z_recv, half_send, mid_recv, mid_half_recv,
):
    row, col = lax.axis_index("row"), lax.axis_index("col")
    y, k, z, x = row // 2, row % 2, col // NX, col % NX

    def at(dy=0, flip=False, dz=0, dx=0):
        core = 1 - k if flip else k
        return (((y + dy + NY) % NY) * 2 + core, ((z + dz + NZ) % NZ) * NX + (x + dx + NX) % NX)

    def send(src, dst, ssem, rsem, device):
        pltpu.make_async_remote_copy(
            src_ref=src, dst_ref=dst, send_sem=ssem, recv_sem=rsem, device_id=device, device_id_type=MESH
        ).start()

    def wait(ref, sem):
        pltpu.make_async_copy(ref, ref, sem).wait()

    def sub(j):
        return pl.ds(pl.multiple_of(((x + j + NX) % NX) * SUB, SUB), SUB)

    def chunk(ch):
        return pl.ds(pl.multiple_of(k * HALF + ch * SUB, SUB), SUB)

    def other_chunk(ch):
        return pl.ds(pl.multiple_of((1 - k) * HALF + ch * SUB, SUB), SUB)

    def block_of(s):
        return (y + offset(s) + 2 * NY) % NY

    own = i_all.at[z, sub(0)]
    loads = [
        pltpu.make_async_copy(src, dst, load.at[n])
        for n, (src, dst) in enumerate(((inp, own), (pre_hbm, pre), (grad_hbm, grad), (w_hbm, w)))
    ]
    for copy in loads:
        copy.start()

    barrier = pltpu.get_barrier_semaphore()
    peers = [at(dz=d) for d in (1, -1, 2, -2)] + [at(dx=d) for d in (1, 2, 3)]
    peers += [at(dy=1), at(dy=-1), at(flip=True)]
    for peer in peers:
        pl.semaphore_signal(barrier, inc=1, device_id=peer, device_id_type=MESH)
    loads[0].wait()
    pl.semaphore_wait(barrier, len(peers))

    send(own, own, iz_own.at[0, 0], iz_recv.at[0, 0], at(dz=1))
    send(own, own, iz_own.at[1, 0], iz_recv.at[1, 0], at(dz=-1))
    for j in (1, 3, 2):
        send(own, own, ix_send.at[j], ix_recv.at[NX - j], at(dx=j))

    loads[1].wait()
    loads[2].wait()
    for ch in range(2):

        @pl.loop(0, SUB // 16)
        def _(r):
            src = pl.ds(pl.multiple_of(ch * SUB + r * 16, 16), 16)
            dst = pl.ds(pl.multiple_of(k * HALF + ch * SUB + r * 16, 16), 16)
            g_all[y, dst, :] = gelu_back(pre[src, :], grad[src, :])

        mine = g_all.at[y, chunk(ch)]
        send(mine, mine, y_own.at[0, ch], y_recv.at[0, 0, ch], at(dy=1))
        send(mine, mine, y_own.at[1, ch], y_recv.at[1, 0, ch], at(dy=-1))
        send(mine, mine, c_send.at[0, ch], c_recv.at[0, ch], at(flip=True))

    acc[...] = jnp.zeros_like(acc)
    loads[3].wait()

    def spread(v):
        return (2 * v + 1) // 3, (v >= 0) & (v <= 11) & (v % 3 != 1)

    @pl.loop(1, 22)
    def _(e):
        @pl.when((e == 1) | ((e >= 3) & (e <= 9)))
        def _():
            s = jnp.maximum(e - 2, 0)
            t = block_of(s)
            for ch in range(2):
                wait(g_all.at[t, other_chunk(ch)], c_recv.at[s, ch])
            part[s] = lax.dot_general(
                g_all[t], w[...], (((1,), (1,)), ((), ())), preferred_element_type=jnp.float32
            ).astype(jnp.bfloat16)
            send(part.at[s, sub(2), pl.ds(0, DH)], half_in.at[s, 0], h_send.at[s, 0], h_recv.at[s, 0], at(dx=1))
            send(part.at[s, sub(2), pl.ds(DH, DH)], half_in.at[s, 1], h_send.at[s, 1], h_recv.at[s, 1], at(dx=-1))

        @pl.when(e <= 7)
        def _():
            hop = (e + 1) // 2
            for way in range(2):
                ch = jnp.where(e == 7, way, (e - 1) % 2)
                s = jnp.minimum(2 * hop - 1 + way, 7)
                block = g_all.at[(y - hop * (1 - 2 * way) + NY) % NY, chunk(ch)]
                wait(block, y_recv.at[way, hop - 1, ch])
                onward = (hop <= 2) | ((hop == 3) & (ch == way))

                @pl.when(onward)
                def _():
                    send(block, block, y_send.at[way, hop, ch], y_recv.at[way, hop, ch], at(dy=1 - 2 * way))

                send(block, block, c_send.at[s, ch], c_recv.at[s, ch], at(flip=True))

        b, due = spread(e - 2)

        @pl.when(due)
        def _():
            for way in range(2):
                wait(half_in.at[b, way], h_recv.at[b, way])
                dest = sub(1 - 2 * way)
                lo, hi = pl.ds(way * DH, DH), pl.ds((1 - way) * DH, DH)
                full_out[b, way, :, lo] = (
                    part[b, dest, lo].astype(jnp.float32) + half_in[b, way].astype(jnp.float32)
                ).astype(jnp.bfloat16)
                full_out[b, way, :, hi] = part[b, dest, hi]
                send(full_out.at[b, way], full_in.at[b, way], f_send.at[b, way], f_recv.at[b, way], at(dx=1 - 2 * way))

        b3, due3 = spread(e - 5)

        @pl.when(due3)
        def _():
            owner = block_of(b3)
            ahead = (owner - z + NZ) % NZ
            for way in range(2):
                wait(full_in.at[b3, way], f_recv.at[b3, way])
            total = part[b3, sub(0), :].astype(jnp.float32)
            total = total + full_in[b3, 0].astype(jnp.float32) + full_in[b3, 1].astype(jnp.float32)
            reduced[owner] = total.astype(jnp.bfloat16)
            whole = reduced.at[owner]
            for way in range(2):

                @pl.when(ahead == (1, 7)[way])
                def _():
                    send(whole, z_in.at[way], z_send.at[way, 0], z_recv.at[way], at(dz=1 - 2 * way))

                @pl.when(ahead == (3, 5)[way])
                def _():
                    send(whole, mid_full.at[way], z_send.at[way, 1], mid_recv.at[way], at(dz=1 - 2 * way))

                @pl.when(ahead == 4)
                def _():
                    half = reduced.at[owner, :, pl.ds(way * DH, DH)]
                    send(half, mid_half.at[way], half_send.at[way], mid_half_recv.at[way], at(dz=2 - 4 * way))

        b4, due4 = spread(e - 8)

        @pl.when(due4)
        def _():
            owner = block_of(b4)
            ahead = (owner - z + NZ) % NZ
            for way in range(2):

                @pl.when(ahead == (2, 6)[way])
                def _():
                    wait(mid_full.at[way], mid_recv.at[way])
                    wait(mid_half.at[way], mid_half_recv.at[way])
                    lo, hi = pl.ds(way * DH, DH), pl.ds((1 - way) * DH, DH)
                    mid_out[way, :, lo] = (
                        reduced[owner, :, lo].astype(jnp.float32)
                        + mid_full[way, :, lo].astype(jnp.float32)
                        + mid_half[way].astype(jnp.float32)
                    ).astype(jnp.bfloat16)
                    mid_out[way, :, hi] = (
                        reduced[owner, :, hi].astype(jnp.float32) + mid_full[way, :, hi].astype(jnp.float32)
                    ).astype(jnp.bfloat16)
                    send(mid_out.at[way], z_in.at[2 + way], z_send.at[way, 2], z_recv.at[2 + way], at(dz=2 - 4 * way))

        def from_x(j):
            block = i_all.at[z, sub(j)]
            wait(block, ix_recv.at[j])
            send(block, block, iz_own.at[0, j], iz_recv.at[0, j], at(dz=1))
            send(block, block, iz_own.at[1, j], iz_recv.at[1, j], at(dz=-1))

        @pl.when(e == 1)
        def _():
            from_x(1)
            from_x(3)

        @pl.when(e == 2)
        def _():
            from_x(2)

        late, due5 = spread(e - 8)
        u = jnp.where(e <= 6, e - 1, 6 + late)

        @pl.when((e <= 6) | due5)
        def _():
            zhop = u // 4 + 1
            for way in range(2):
                j = order(u % 4 + jnp.where(zhop == 4, 2 * way, 0))
                rank = u % 4 + jnp.where(zhop == 4, 2 * way, 0)
                block = i_all.at[(z - zhop * (1 - 2 * way) + NZ) % NZ, sub(j)]
                wait(block, iz_recv.at[way, zhop * 4 - 4 + j])
                onward = (zhop <= 2) | ((zhop == 3) & (rank // 2 == way))

                @pl.when(onward)
                def _():
                    send(block, block, iz_send.at[way, u], iz_recv.at[way, zhop * 4 + j], at(dz=1 - 2 * way))

        @pl.when(((e >= 10) & (e <= 14)) | (e == 17) | (e == 18) | (e == 21))
        def _():
            q = e - 10 - jnp.where(e >= 17, 2, 0) - jnp.where(e >= 21, 2, 0)
            b = (z + offset(q) + 2 * NZ) % NZ
            for n in range(3):
                cols = pl.ds(n * 256, 256)
                acc[cols, :] += lax.dot_general(
                    i_all[b, :, cols], g_all[b], (((0,), (0,)), ((), ())), preferred_element_type=jnp.float32
                )

    @pl.loop(0, D // 32)
    def _(r):
        rows = pl.ds(pl.multiple_of(r * 32, 32), 32)
        wg[rows, :] = acc[rows, :].astype(jnp.bfloat16)

    for n in range(4):
        wait(z_in.at[n], z_recv.at[n])

    @pl.loop(0, SUB // 16)
    def _(r):
        rows = pl.ds(pl.multiple_of(r * 16, 16), 16)
        total = reduced[z, rows, :].astype(jnp.float32)
        for n in range(4):
            total = total + z_in[n, rows, :].astype(jnp.float32)
        ig[rows, :] = total.astype(jnp.bfloat16)

    shard = i_all.at[0, pl.ds(0, SUB)]
    for j in (1, 2, 3):
        wait(shard, ix_send.at[j])
    for way in range(2):
        for j in range(4):
            wait(shard, iz_own.at[way, j])
        for u in range(8):
            wait(shard, iz_send.at[way, u])
        for j in range(2):
            wait(shard, iz_send.at[way, 8 + 2 * way + j])
        for ch in range(2):
            wait(shard, y_own.at[way, ch])
            for hop in (1, 2):
                wait(shard, y_send.at[way, hop, ch])
        wait(shard, y_send.at[way, 3, way])
        for n in range(3):
            wait(shard, z_send.at[way, n])
        wait(mid_half.at[way], half_send.at[way])
    for s in range(8):
        for ch in range(2):
            wait(shard, c_send.at[s, ch])
        for way in range(2):
            wait(half_in.at[0, 0], h_send.at[s, way])
            wait(shard, f_send.at[s, way])


def order(n):
    return jnp.where(n >= 2, 5 - n, n)


def on_device(inputs, pre_act, grad_act, up_weight):
    bf16 = jnp.bfloat16
    dma = pltpu.SemaphoreType.DMA
    vmem = pl.BlockSpec(memory_space=pltpu.VMEM)
    return tuple(
        pl.pallas_call(
            kernel,
            out_shape=(jax.ShapeDtypeStruct((SUB, D), bf16), jax.ShapeDtypeStruct((D, F), bf16)),
            in_specs=[pl.BlockSpec(memory_space=pl.ANY)] * 4,
            out_specs=(vmem, vmem),
            scratch_shapes=[
                pltpu.VMEM((HALF, F), bf16),
                pltpu.VMEM((HALF, F), bf16),
                pltpu.VMEM((D, F), bf16),
                pltpu.VMEM((NZ, BLOCK, D), bf16),
                pltpu.VMEM((NY, BLOCK, F), bf16),
                pltpu.VMEM((8, BLOCK, D), bf16),
                pltpu.VMEM((8, 2, SUB, DH), bf16),
                pltpu.VMEM((8, 2, SUB, D), bf16),
                pltpu.VMEM((8, 2, SUB, D), bf16),
                pltpu.VMEM((NZ, SUB, D), bf16),
                pltpu.VMEM((2, SUB, D), bf16),
                pltpu.VMEM((2, SUB, DH), bf16),
                pltpu.VMEM((2, SUB, D), bf16),
                pltpu.VMEM((4, SUB, D), bf16),
                pltpu.VMEM((D, F), jnp.float32),
                dma((4,)), dma((2, 2)), dma((2, 4, 2)), dma((2, 4, 2)), dma((8, 2)), dma((8, 2)),
                dma((4,)), dma((4,)), dma((2, 4)), dma((2, 12)), dma((2, 16)),
                dma((8, 2)), dma((8, 2)), dma((8, 2)), dma((8, 2)),
                dma((2, 3)), dma((4,)), dma((2,)), dma((2,)), dma((2,)),
            ],
            compiler_params=pltpu.CompilerParams(
                collective_id=0, has_side_effects=True, vmem_limit_bytes=60 * 2**20
            ),
            cost_estimate=pl.CostEstimate(flops=4 * 2048 * D * F, bytes_accessed=6 * 2**20, transcendentals=HALF * F),
            name="up_gelu_backward",
        )(inputs, pre_act, grad_act, up_weight)
    )


def solution(mesh):
    placed = (P("col", "row"), P("row", "col"), P("row", "col"), P("row", "col"))
    return jax.shard_map(
        on_device,
        mesh=mesh,
        in_specs=placed,
        out_specs=(P("col", "row"), P("row", "col")),
        check_vma=False,
    )
```

```python
import functools
import math

import jax
import jax.numpy as jnp
from jax import lax
from jax.experimental import pallas as pl
from jax.experimental.pallas import tpu as pltpu
from jax.sharding import PartitionSpec as P

MESH = pl.DeviceIdType.MESH
curve = math.sqrt(2.0 / math.pi)
cubic = 0.044715

NY, NZ, NX = 8, 8, 4
SUB = 64
BLOCK = 256
HALF = 128
D = 768
F = 768
DH = D // 2


def gelu_back(pre_act, grad_act):
    h = pre_act.astype(jnp.float32)
    t = jnp.tanh(curve * (h + cubic * h * h * h))
    slope = 0.5 * (1.0 + t) + 0.5 * h * (1.0 - t * t) * curve * (1.0 + 3.0 * cubic * h * h)
    return (grad_act.astype(jnp.float32) * slope).astype(jnp.bfloat16)


ORDER = (
    (0, 1, 7, 2, 3, 4, 5, 6),
    (1, 0, 2, 3, 4, 5, 6, 7),
    (2, 1, 3, 0, 4, 5, 6, 7),
    (3, 2, 4, 1, 0, 5, 6, 7),
    (4, 3, 5, 2, 1, 0, 6, 7),
    (5, 4, 6, 3, 0, 1, 2, 7),
    (6, 5, 7, 0, 1, 2, 3, 4),
    (7, 0, 6, 1, 2, 3, 4, 5),
)
MATMUL_AT = (1, 3, 4, 5, 7, 9, 10, 11)
HALF_AT = (2, 4, 5, 7, 8, 11, 12, 13)
FULL_AT = (5, 7, 8, 10, 11, 13, 14, 15)
SHARD_AT = (1, 3, 4, 5, 6, 7, 8, 10, 11, 13, 14, 16, 17)
MID_AT = (8, 10, 11, 13, 14, 16, 17, 18)


def turn(e, steps):
    index, due = 0, e == steps[0]
    for n in range(1, len(steps)):
        index = jnp.where(e >= steps[n], n, index)
        due = due | (e == steps[n])
    return index, due


def offset(s):
    return jnp.where(s % 2 == 1, -((s + 1) // 2), s // 2)


def kernel(
    inp, g_own, w_hbm, ig, wg,
    w, i_all, g_all, part, half_in, full_in, full_out, reduced, mid_full, mid_half, mid_out, z_in, acc,
    load, y_own, y_send, y_recv, c_send, c_recv, ix_send, ix_recv, iz_own, iz_send, iz_recv,
    h_send, h_recv, f_send, f_recv, z_send, z_recv, half_send, mid_recv, mid_half_recv,
):
    row, col = lax.axis_index("row"), lax.axis_index("col")
    y, k, z, x = row // 2, row % 2, col // NX, col % NX

    def at(dy=0, flip=False, dz=0, dx=0):
        core = 1 - k if flip else k
        return (((y + dy + NY) % NY) * 2 + core, ((z + dz + NZ) % NZ) * NX + (x + dx + NX) % NX)

    def send(src, dst, ssem, rsem, device):
        pltpu.make_async_remote_copy(
            src_ref=src, dst_ref=dst, send_sem=ssem, recv_sem=rsem, device_id=device, device_id_type=MESH
        ).start()

    def wait(ref, sem):
        pltpu.make_async_copy(ref, ref, sem).wait()

    def sub(j):
        return pl.ds(pl.multiple_of(((x + j + NX) % NX) * SUB, SUB), SUB)

    def chunk(ch):
        return pl.ds(pl.multiple_of(k * HALF + ch * SUB, SUB), SUB)

    def other_chunk(ch):
        return pl.ds(pl.multiple_of((1 - k) * HALF + ch * SUB, SUB), SUB)

    places = pick(y, [sum(t << (3 * s) for s, t in enumerate(order)) for order in ORDER])

    def block_of(s):
        return lax.shift_right_logical(places, 3 * s) & 7

    w_load = pltpu.make_async_copy(w_hbm, w, load)
    w_load.start()

    barrier = pltpu.get_barrier_semaphore()
    peers = [at(dz=d) for d in (1, -1, 2, -2)] + [at(dx=d) for d in (1, 2, 3)]
    peers += [at(dy=1), at(dy=-1), at(flip=True)]
    for peer in peers:
        pl.semaphore_signal(barrier, inc=1, device_id=peer, device_id_type=MESH)
    pl.semaphore_wait(barrier, len(peers))

    own = i_all.at[z, sub(0)]
    for ch in range(2):
        mine, there = g_own.at[pl.ds(ch * SUB, SUB)], g_all.at[y, chunk(ch)]
        send(mine, there, y_own.at[0, ch], y_recv.at[0, 0, ch], at(dy=1))
        send(mine, there, y_own.at[1, ch], y_recv.at[1, 0, ch], at(dy=-1))
        send(mine, there, c_send.at[0, ch], c_recv.at[0, ch], at(flip=True))
        if ch == 0:
            send(inp, own, iz_own.at[0, 0], iz_recv.at[0, 0], at(dz=1))
            send(inp, own, iz_own.at[1, 0], iz_recv.at[1, 0], at(dz=-1))
            for j in (1, 3, 2):
                send(inp, own, ix_send.at[j], ix_recv.at[NX - j], at(dx=j))

    i_all[z, sub(0), :] = inp[...]
    g_all[y, pl.ds(pl.multiple_of(k * HALF, HALF), HALF), :] = g_own[...]
    acc[...] = jnp.zeros_like(acc)
    w_load.wait()

    @pl.loop(1, 21)
    def _(e):
        s, due1 = turn(e, MATMUL_AT)

        @pl.when(due1)
        def _():
            t = block_of(s)
            ahead = (t - y + NY) % NY
            arrival = jnp.where(ahead <= 3, 2 * ahead, 2 * (NY - ahead) - 1)
            for ch in range(2):
                wait(g_all.at[t, other_chunk(ch)], c_recv.at[arrival, ch])
            part[s] = lax.dot_general(
                g_all[t], w[...], (((1,), (1,)), ((), ())), preferred_element_type=jnp.float32
            ).astype(jnp.bfloat16)
            send(part.at[s, sub(2), pl.ds(0, DH)], half_in.at[s, 0], h_send.at[s, 0], h_recv.at[s, 0], at(dx=1))
            send(part.at[s, sub(2), pl.ds(DH, DH)], half_in.at[s, 1], h_send.at[s, 1], h_recv.at[s, 1], at(dx=-1))

        @pl.when(e <= 7)
        def _():
            hop = (e + 1) // 2
            for way in range(2):
                ch = jnp.where(e == 7, way, (e - 1) % 2)
                s = jnp.minimum(2 * hop - 1 + way, 7)
                block = g_all.at[(y - hop * (1 - 2 * way) + NY) % NY, chunk(ch)]
                wait(block, y_recv.at[way, hop - 1, ch])
                onward = (hop <= 2) | ((hop == 3) & (ch == way))

                @pl.when(onward)
                def _():
                    send(block, block, y_send.at[way, hop, ch], y_recv.at[way, hop, ch], at(dy=1 - 2 * way))

                send(block, block, c_send.at[s, ch], c_recv.at[s, ch], at(flip=True))

        b, due = turn(e, HALF_AT)

        @pl.when(due)
        def _():
            for way in range(2):
                wait(half_in.at[b, way], h_recv.at[b, way])
                dest = sub(1 - 2 * way)
                lo, hi = pl.ds(way * DH, DH), pl.ds((1 - way) * DH, DH)
                full_out[b, way, :, lo] = (
                    part[b, dest, lo].astype(jnp.float32) + half_in[b, way].astype(jnp.float32)
                ).astype(jnp.bfloat16)
                full_out[b, way, :, hi] = part[b, dest, hi]
                send(full_out.at[b, way], full_in.at[b, way], f_send.at[b, way], f_recv.at[b, way], at(dx=1 - 2 * way))

        b3, due3 = turn(e, FULL_AT)

        @pl.when(due3)
        def _():
            owner = block_of(b3)
            ahead = (owner - z + NZ) % NZ
            for way in range(2):
                wait(full_in.at[b3, way], f_recv.at[b3, way])
            total = part[b3, sub(0), :].astype(jnp.float32)
            total = total + full_in[b3, 0].astype(jnp.float32) + full_in[b3, 1].astype(jnp.float32)
            reduced[owner] = total.astype(jnp.bfloat16)
            whole = reduced.at[owner]
            for way in range(2):

                @pl.when(ahead == (1, 7)[way])
                def _():
                    send(whole, z_in.at[way], z_send.at[way, 0], z_recv.at[way], at(dz=1 - 2 * way))

                @pl.when(ahead == (3, 5)[way])
                def _():
                    send(whole, mid_full.at[way], z_send.at[way, 1], mid_recv.at[way], at(dz=1 - 2 * way))

                @pl.when(ahead == 4)
                def _():
                    half = reduced.at[owner, :, pl.ds(way * DH, DH)]
                    send(half, mid_half.at[way], half_send.at[way], mid_half_recv.at[way], at(dz=2 - 4 * way))

        b4, due4 = turn(e, MID_AT)

        @pl.when(due4)
        def _():
            owner = block_of(b4)
            ahead = (owner - z + NZ) % NZ
            for way in range(2):

                @pl.when(ahead == (2, 6)[way])
                def _():
                    wait(mid_full.at[way], mid_recv.at[way])
                    wait(mid_half.at[way], mid_half_recv.at[way])
                    lo, hi = pl.ds(way * DH, DH), pl.ds((1 - way) * DH, DH)
                    mid_out[way, :, lo] = (
                        reduced[owner, :, lo].astype(jnp.float32)
                        + mid_full[way, :, lo].astype(jnp.float32)
                        + mid_half[way].astype(jnp.float32)
                    ).astype(jnp.bfloat16)
                    mid_out[way, :, hi] = (
                        reduced[owner, :, hi].astype(jnp.float32) + mid_full[way, :, hi].astype(jnp.float32)
                    ).astype(jnp.bfloat16)
                    send(mid_out.at[way], z_in.at[2 + way], z_send.at[way, 2], z_recv.at[2 + way], at(dz=2 - 4 * way))

        def from_x(j):
            block = i_all.at[z, sub(j)]
            wait(block, ix_recv.at[j])
            send(block, block, iz_own.at[0, j], iz_recv.at[0, j], at(dz=1))
            send(block, block, iz_own.at[1, j], iz_recv.at[1, j], at(dz=-1))

        u, due5 = turn(e, SHARD_AT)

        @pl.when(due5)
        def _():
            zhop = pick(u, (1, 2, 1, 3, 1, 4, 1, 2, 2, 2, 3, 3, 3))
            j = pick(u, (0, 0, 1, 0, 3, 0, 2, 1, 3, 2, 1, 3, 2))
            for way in range(2):
                owner = (z - zhop * (1 - 2 * way) + NZ) % NZ
                block = i_all.at[owner, sub(j)]
                half = i_all.at[owner, pl.ds(pl.multiple_of(x * SUB + way * (SUB // 2), SUB // 2), SUB // 2)]

                @pl.when(zhop <= 3)
                def _():
                    wait(block, iz_recv.at[way, zhop * 4 - 4 + j])

                @pl.when(zhop == 4)
                def _():
                    wait(half, iz_recv.at[way, 12])

                @pl.when(zhop <= 2)
                def _():
                    send(block, block, iz_send.at[way, u], iz_recv.at[way, zhop * 4 + j], at(dz=1 - 2 * way))

                @pl.when((zhop == 3) & (j == 0))
                def _():
                    send(half, half, iz_send.at[way, u], iz_recv.at[way, 12], at(dz=1 - 2 * way))

        for step, j in ((1, 1), (2, 3), (4, 2)):

            @pl.when(e == step)
            def _():
                from_x(j)

        @pl.when(e == 13)
        def _():
            block = i_all.at[(z + 4) % NZ, sub(0)]
            for j in (1, 3, 2):
                send(block, block, ix_send.at[3 + j], ix_recv.at[3 + NX - j], at(dx=j))

        @pl.when(e == 18)
        def _():
            for j in (1, 3, 2):
                wait(i_all.at[(z + 4) % NZ, sub(j)], ix_recv.at[3 + j])

        @pl.when(((e >= 11) & (e <= 15)) | (e >= 18))
        def _():
            q = jnp.where(e <= 15, e - 11, jnp.where(e == 18, 7, e - 14))
            b = (z + offset(q) + 2 * NZ) % NZ
            for n in range(3):
                cols = pl.ds(n * 256, 256)
                acc[cols, :] += lax.dot_general(
                    i_all[b, :, cols], g_all[b], (((0,), (0,)), ((), ())), preferred_element_type=jnp.float32
                )

    @pl.loop(0, D // 32)
    def _(r):
        rows = pl.ds(pl.multiple_of(r * 32, 32), 32)
        wg[rows, :] = acc[rows, :].astype(jnp.bfloat16)

    for n in range(4):
        wait(z_in.at[n], z_recv.at[n])

    @pl.loop(0, SUB // 16)
    def _(r):
        rows = pl.ds(pl.multiple_of(r * 16, 16), 16)
        total = reduced[z, rows, :].astype(jnp.float32)
        for n in range(4):
            total = total + z_in[n, rows, :].astype(jnp.float32)
        ig[rows, :] = total.astype(jnp.bfloat16)

    shard = i_all.at[0, pl.ds(0, SUB)]
    for j in range(1, 7):
        wait(shard, ix_send.at[j])
    for way in range(2):
        for j in range(4):
            wait(shard, iz_own.at[way, j])
        for u in (0, 1, 2, 4, 6, 7, 8, 9):
            wait(shard, iz_send.at[way, u])
        wait(i_all.at[0, pl.ds(0, SUB // 2)], iz_send.at[way, 3])
        for ch in range(2):
            wait(shard, y_own.at[way, ch])
            for hop in (1, 2):
                wait(shard, y_send.at[way, hop, ch])
        wait(shard, y_send.at[way, 3, way])
        for n in range(3):
            wait(shard, z_send.at[way, n])
        wait(mid_half.at[way], half_send.at[way])
    for s in range(8):
        for ch in range(2):
            wait(shard, c_send.at[s, ch])
        for way in range(2):
            wait(half_in.at[0, 0], h_send.at[s, way])
            wait(shard, f_send.at[s, way])


def pick(n, table):
    value = table[-1]
    for m in range(len(table) - 1):
        value = jnp.where(n == m, table[m], value)
    return value


def on_device(inputs, pre_act, grad_act, up_weight):
    bf16 = jnp.bfloat16
    dma = pltpu.SemaphoreType.DMA
    vmem = pl.BlockSpec(memory_space=pltpu.VMEM)
    return tuple(
        pl.pallas_call(
            kernel,
            out_shape=(jax.ShapeDtypeStruct((SUB, D), bf16), jax.ShapeDtypeStruct((D, F), bf16)),
            in_specs=[vmem, vmem, pl.BlockSpec(memory_space=pltpu.HBM)],
            out_specs=(vmem, vmem),
            scratch_shapes=[
                pltpu.VMEM((D, F), bf16),
                pltpu.VMEM((NZ, BLOCK, D), bf16),
                pltpu.VMEM((NY, BLOCK, F), bf16),
                pltpu.VMEM((8, BLOCK, D), bf16),
                pltpu.VMEM((8, 2, SUB, DH), bf16),
                pltpu.VMEM((8, 2, SUB, D), bf16),
                pltpu.VMEM((8, 2, SUB, D), bf16),
                pltpu.VMEM((NZ, SUB, D), bf16),
                pltpu.VMEM((2, SUB, D), bf16),
                pltpu.VMEM((2, SUB, DH), bf16),
                pltpu.VMEM((2, SUB, D), bf16),
                pltpu.VMEM((4, SUB, D), bf16),
                pltpu.VMEM((D, F), jnp.float32),
                dma, dma((2, 2)), dma((2, 4, 2)), dma((2, 4, 2)), dma((8, 2)), dma((8, 2)),
                dma((7,)), dma((7,)), dma((2, 4)), dma((2, 10)), dma((2, 13)),
                dma((8, 2)), dma((8, 2)), dma((8, 2)), dma((8, 2)),
                dma((2, 3)), dma((4,)), dma((2,)), dma((2,)), dma((2,)),
            ],
            compiler_params=pltpu.CompilerParams(
                collective_id=0, has_side_effects=True, vmem_limit_bytes=52 * 2**20
            ),
            cost_estimate=pl.CostEstimate(flops=4 * 2048 * D * F, bytes_accessed=6 * 2**20, transcendentals=0),
            name="up_gelu_backward",
        )(inputs, gelu_back(pre_act, grad_act), up_weight)
    )


def solution(mesh):
    placed = (P("col", "row"), P("row", "col"), P("row", "col"), P("row", "col"))
    return jax.shard_map(
        on_device,
        mesh=mesh,
        in_specs=placed,
        out_specs=(P("col", "row"), P("row", "col")),
        check_vma=False,
    )
```

```python
import functools
import math

import jax
import jax.numpy as jnp
from jax import lax
from jax.experimental import pallas as pl
from jax.experimental.pallas import tpu as pltpu
from jax.sharding import PartitionSpec as P

MESH = pl.DeviceIdType.MESH
curve = math.sqrt(2.0 / math.pi)
cubic = 0.044715

NY, NZ, NX = 8, 8, 4
SUB = 64
BLOCK = 256
HALF = 128
D = 768
F = 768
DH = D // 2


def gelu_back(pre_act, grad_act):
    h = pre_act.astype(jnp.float32)
    t = jnp.tanh(curve * (h + cubic * h * h * h))
    slope = 0.5 * (1.0 + t) + 0.5 * h * (1.0 - t * t) * curve * (1.0 + 3.0 * cubic * h * h)
    return (grad_act.astype(jnp.float32) * slope).astype(jnp.bfloat16)


ORDER = (
    (0, 1, 7, 2, 3, 4, 5, 6),
    (1, 0, 2, 3, 4, 5, 6, 7),
    (2, 1, 3, 0, 4, 5, 6, 7),
    (3, 2, 4, 1, 0, 5, 6, 7),
    (4, 3, 5, 2, 1, 0, 6, 7),
    (5, 4, 6, 3, 0, 1, 2, 7),
    (6, 5, 7, 0, 1, 2, 3, 4),
    (7, 0, 6, 1, 2, 3, 4, 5),
)
MATMUL_AT = (1, 3, 4, 5, 7, 9, 10, 11)
HALF_AT = (3, 5, 6, 7, 9, 11, 12, 13)
FULL_AT = (5, 7, 8, 10, 12, 13, 14, 15)
SHARD_AT = (1, 3, 4, 5, 6, 7, 8, 10, 11, 13, 14, 16, 17)
MID_AT = (8, 10, 11, 13, 15, 16, 17, 18)


def turn(e, steps):
    index, due = 0, e == steps[0]
    for n in range(1, len(steps)):
        index = jnp.where(e >= steps[n], n, index)
        due = due | (e == steps[n])
    return index, due


def offset(s):
    return jnp.where((s & 1) == 1, -lax.shift_right_logical(s + 1, 1), lax.shift_right_logical(s, 1))


def kernel(
    inp, pre_hbm, grad_hbm, w_hbm, ig, wg,
    pre, grad, w, i_all, g_all, part, half_in, full_in, full_out, reduced, mid_full, mid_half, mid_out, z_in, acc,
    load, y_own, y_send, y_recv, c_send, c_recv, ix_send, ix_recv, ix_half_send, ix_half_recv, iz_own, iz_send, iz_recv,
    h_send, h_recv, g_send, g_recv, f_send, f_recv, z_send, z_recv, half_send, mid_recv, mid_half_recv,
):
    row, col = lax.axis_index("row"), lax.axis_index("col")
    y, k, z, x = row // 2, row & 1, col // NX, col & (NX - 1)

    def at(dy=0, flip=False, dz=0, dx=0):
        core = 1 - k if flip else k
        return (((y + dy) & (NY - 1)) * 2 + core, ((z + dz) & (NZ - 1)) * NX + ((x + dx) & (NX - 1)))

    def send(src, dst, ssem, rsem, device):
        pltpu.make_async_remote_copy(
            src_ref=src, dst_ref=dst, send_sem=ssem, recv_sem=rsem, device_id=device, device_id_type=MESH
        ).start()

    def wait(ref, sem):
        pltpu.make_async_copy(ref, ref, sem).wait()

    def sub(j):
        return pl.ds(pl.multiple_of(((x + j) & (NX - 1)) * SUB, SUB), SUB)

    def chunk(ch):
        return pl.ds(pl.multiple_of(k * HALF + ch * SUB, SUB), SUB)

    def other_chunk(ch):
        return pl.ds(pl.multiple_of((1 - k) * HALF + ch * SUB, SUB), SUB)

    places = pick(y, [sum(t << (3 * s) for s, t in enumerate(order)) for order in ORDER])

    def block_of(s):
        return lax.shift_right_logical(places, 3 * s) & 7

    own = i_all.at[z, sub(0)]
    pre_load = pltpu.make_async_copy(pre_hbm, pre, load.at[0])
    grad_load = pltpu.make_async_copy(grad_hbm, grad, load.at[1])
    inp_load = pltpu.make_async_copy(inp, own, load.at[2])
    w_load = pltpu.make_async_copy(w_hbm, w, load.at[3])
    for copy in (pre_load, grad_load, inp_load, w_load):
        copy.start()

    barrier = pltpu.get_barrier_semaphore()
    peers = [at(dz=d) for d in (1, -1, 2, -2)] + [at(dx=d) for d in (1, 2, 3)]
    peers += [at(dy=1), at(dy=-1), at(flip=True)]
    for peer in peers:
        pl.semaphore_signal(barrier, inc=1, device_id=peer, device_id_type=MESH)
    pre_load.wait()
    grad_load.wait()
    for ch in range(2):

        @pl.loop(0, SUB // 16)
        def _(r):
            src = pl.ds(pl.multiple_of(ch * SUB + r * 16, 16), 16)
            dst = pl.ds(pl.multiple_of(k * HALF + ch * SUB + r * 16, 16), 16)
            g_all[y, dst, :] = gelu_back(pre[src, :], grad[src, :])

        if ch == 0:
            pl.semaphore_wait(barrier, len(peers))
        mine = g_all.at[y, chunk(ch)]
        send(mine, mine, y_own.at[0, ch], y_recv.at[0, 0, ch], at(dy=1))
        send(mine, mine, y_own.at[1, ch], y_recv.at[1, 0, ch], at(dy=-1))
        send(mine, mine, c_send.at[0, ch], c_recv.at[0, ch], at(flip=True))
        if ch == 0:
            inp_load.wait()
            send(own, own, iz_own.at[0, 0], iz_recv.at[0, 0], at(dz=1))
            send(own, own, iz_own.at[1, 0], iz_recv.at[1, 0], at(dz=-1))
            for j in (1, 3):
                send(own, own, ix_send.at[j], ix_recv.at[NX - j], at(dx=j))

    acc[...] = jnp.zeros_like(acc)
    w_load.wait()

    @pl.loop(1, 21)
    def _(e):
        s, due1 = turn(e, MATMUL_AT)

        @pl.when(due1)
        def _():
            t = block_of(s)
            ahead = (t - y) & (NY - 1)
            arrival = jnp.where(ahead <= 3, 2 * ahead, 2 * (NY - ahead) - 1)
            for ch in range(2):
                wait(g_all.at[t, other_chunk(ch)], c_recv.at[arrival, ch])
            part[s] = lax.dot_general(
                g_all[t], w[...], (((1,), (1,)), ((), ())), preferred_element_type=jnp.float32
            ).astype(jnp.bfloat16)
            send(part.at[s, sub(2), pl.ds(0, DH)], half_in.at[s, 0], h_send.at[s, 0], h_recv.at[s, 0], at(dx=1))
            send(part.at[s, sub(2), pl.ds(DH, DH)], half_in.at[s, 1], h_send.at[s, 1], h_recv.at[s, 1], at(dx=-1))
            for way in range(2):
                hi = pl.ds((1 - way) * DH, DH)
                send(
                    part.at[s, sub(1 - 2 * way), hi], full_in.at[s, way, :, hi],
                    g_send.at[s, way], g_recv.at[s, way], at(dx=1 - 2 * way),
                )

        @pl.when(e <= 7)
        def _():
            hop = lax.shift_right_logical(e + 1, 1)
            for way in range(2):
                ch = jnp.where(e == 7, way, (e - 1) & 1)
                s = jnp.minimum(2 * hop - 1 + way, 7)
                block = g_all.at[(y - hop * (1 - 2 * way)) & (NY - 1), chunk(ch)]
                wait(block, y_recv.at[way, hop - 1, ch])
                onward = (hop <= 2) | ((hop == 3) & (ch == way))

                @pl.when(onward)
                def _():
                    send(block, block, y_send.at[way, hop, ch], y_recv.at[way, hop, ch], at(dy=1 - 2 * way))

                send(block, block, c_send.at[s, ch], c_recv.at[s, ch], at(flip=True))

        b, due = turn(e, HALF_AT)

        @pl.when(due)
        def _():
            for way in range(2):
                wait(half_in.at[b, way], h_recv.at[b, way])
                dest = sub(1 - 2 * way)
                lo = pl.ds(way * DH, DH)
                full_out[b, way] = (
                    part[b, dest, lo].astype(jnp.float32) + half_in[b, way].astype(jnp.float32)
                ).astype(jnp.bfloat16)
                send(
                    full_out.at[b, way], full_in.at[b, way, :, lo],
                    f_send.at[b, way], f_recv.at[b, way], at(dx=1 - 2 * way),
                )

        b3, due3 = turn(e, FULL_AT)

        @pl.when(due3)
        def _():
            owner = block_of(b3)
            ahead = (owner - z) & (NZ - 1)
            for way in range(2):
                wait(full_in.at[b3, way, :, pl.ds((1 - way) * DH, DH)], g_recv.at[b3, way])
                wait(full_in.at[b3, way, :, pl.ds(way * DH, DH)], f_recv.at[b3, way])
            total = part[b3, sub(0), :].astype(jnp.float32)
            total = total + full_in[b3, 0].astype(jnp.float32) + full_in[b3, 1].astype(jnp.float32)
            reduced[owner] = total.astype(jnp.bfloat16)
            whole = reduced.at[owner]
            for way in range(2):

                @pl.when(ahead == (1, 7)[way])
                def _():
                    send(whole, z_in.at[way], z_send.at[way, 0], z_recv.at[way], at(dz=1 - 2 * way))

                @pl.when(ahead == (3, 5)[way])
                def _():
                    send(whole, mid_full.at[way], z_send.at[way, 1], mid_recv.at[way], at(dz=1 - 2 * way))

                @pl.when(ahead == 4)
                def _():
                    half = reduced.at[owner, :, pl.ds(way * DH, DH)]
                    send(half, mid_half.at[way], half_send.at[way], mid_half_recv.at[way], at(dz=2 - 4 * way))

        b4, due4 = turn(e, MID_AT)

        @pl.when(due4)
        def _():
            owner = block_of(b4)
            ahead = (owner - z) & (NZ - 1)
            for way in range(2):

                @pl.when(ahead == (2, 6)[way])
                def _():
                    wait(mid_full.at[way], mid_recv.at[way])
                    wait(mid_half.at[way], mid_half_recv.at[way])
                    lo, hi = pl.ds(way * DH, DH), pl.ds((1 - way) * DH, DH)
                    mid_out[way, :, lo] = (
                        reduced[owner, :, lo].astype(jnp.float32)
                        + mid_full[way, :, lo].astype(jnp.float32)
                        + mid_half[way].astype(jnp.float32)
                    ).astype(jnp.bfloat16)
                    mid_out[way, :, hi] = (
                        reduced[owner, :, hi].astype(jnp.float32) + mid_full[way, :, hi].astype(jnp.float32)
                    ).astype(jnp.bfloat16)
                    send(mid_out.at[way], z_in.at[2 + way], z_send.at[way, 2], z_recv.at[2 + way], at(dz=2 - 4 * way))

        def quarter(j, way):
            return i_all.at[z, pl.ds(pl.multiple_of(((x + j) & (NX - 1)) * SUB + way * (SUB // 2), SUB // 2), SUB // 2)]

        def from_x(j):
            block = i_all.at[z, sub(j)]
            if j == 2:
                for way in range(2):
                    wait(quarter(2, way), ix_half_recv.at[way])
            else:
                wait(block, ix_recv.at[j])
                way = 0 if j == 3 else 1
                part_of = quarter(j, way)
                send(part_of, part_of, ix_half_send.at[way], ix_half_recv.at[way], at(dx=1 - 2 * way))
            send(block, block, iz_own.at[0, j], iz_recv.at[0, j], at(dz=1))
            send(block, block, iz_own.at[1, j], iz_recv.at[1, j], at(dz=-1))

        u, due5 = turn(e, SHARD_AT)

        @pl.when(due5)
        def _():
            zhop = pick(u, (1, 2, 1, 3, 1, 4, 1, 2, 2, 2, 3, 3, 3))
            j = pick(u, (0, 0, 1, 0, 3, 0, 2, 1, 3, 2, 1, 3, 2))
            for way in range(2):
                owner = (z - zhop * (1 - 2 * way)) & (NZ - 1)
                block = i_all.at[owner, sub(j)]
                half = i_all.at[owner, pl.ds(pl.multiple_of(x * SUB + way * (SUB // 2), SUB // 2), SUB // 2)]

                @pl.when(zhop <= 3)
                def _():
                    wait(block, iz_recv.at[way, zhop * 4 - 4 + j])

                @pl.when(zhop == 4)
                def _():
                    wait(half, iz_recv.at[way, 12])

                @pl.when(zhop <= 2)
                def _():
                    send(block, block, iz_send.at[way, u], iz_recv.at[way, zhop * 4 + j], at(dz=1 - 2 * way))

                @pl.when((zhop == 3) & (j == 0))
                def _():
                    send(half, half, iz_send.at[way, u], iz_recv.at[way, 12], at(dz=1 - 2 * way))

        for step, j in ((1, 1), (2, 3), (4, 2)):

            @pl.when(e == step)
            def _():
                from_x(j)

        @pl.when(e == 13)
        def _():
            block = i_all.at[(z + 4) & (NZ - 1), sub(0)]
            for j in (1, 3, 2):
                send(block, block, ix_send.at[3 + j], ix_recv.at[3 + NX - j], at(dx=j))

        @pl.when(e == 18)
        def _():
            for j in (1, 3, 2):
                wait(i_all.at[(z + 4) & (NZ - 1), sub(j)], ix_recv.at[3 + j])

        @pl.when(((e >= 11) & (e <= 15)) | (e >= 18))
        def _():
            q = jnp.where(e <= 15, e - 11, jnp.where(e == 18, 7, e - 14))
            b = (z + offset(q)) & (NZ - 1)
            for n in range(3):
                cols = pl.ds(n * 256, 256)
                acc[cols, :] += lax.dot_general(
                    i_all[b, :, cols], g_all[b], (((0,), (0,)), ((), ())), preferred_element_type=jnp.float32
                )

    @pl.loop(0, D // 32)
    def _(r):
        rows = pl.ds(pl.multiple_of(r * 32, 32), 32)
        wg[rows, :] = acc[rows, :].astype(jnp.bfloat16)

    shard = i_all.at[0, pl.ds(0, SUB)]
    half_shard = i_all.at[0, pl.ds(0, SUB // 2)]
    for j in (1, 3, 4, 5, 6):
        wait(shard, ix_send.at[j])
    for way in range(2):
        wait(half_shard, ix_half_send.at[way])
        for j in range(4):
            wait(shard, iz_own.at[way, j])
        for u in (0, 1, 2, 4, 6, 7, 8, 9):
            wait(shard, iz_send.at[way, u])
        wait(half_shard, iz_send.at[way, 3])
        for ch in range(2):
            wait(shard, y_own.at[way, ch])
            for hop in (1, 2):
                wait(shard, y_send.at[way, hop, ch])
        wait(shard, y_send.at[way, 3, way])
    for s in range(8):
        for ch in range(2):
            wait(shard, c_send.at[s, ch])
        for way in range(2):
            wait(half_in.at[0, 0], h_send.at[s, way])
            wait(half_in.at[0, 0], g_send.at[s, way])
            wait(half_in.at[0, 0], f_send.at[s, way])

    for n in range(4):
        wait(z_in.at[n], z_recv.at[n])

    @pl.loop(0, SUB // 16)
    def _(r):
        rows = pl.ds(pl.multiple_of(r * 16, 16), 16)
        total = reduced[z, rows, :].astype(jnp.float32)
        for n in range(4):
            total = total + z_in[n, rows, :].astype(jnp.float32)
        ig[rows, :] = total.astype(jnp.bfloat16)

    for way in range(2):
        for n in range(3):
            wait(shard, z_send.at[way, n])
        wait(mid_half.at[way], half_send.at[way])


def pick(n, table):
    value = table[-1]
    for m in range(len(table) - 1):
        value = jnp.where(n == m, table[m], value)
    return value


def on_device(inputs, pre_act, grad_act, up_weight):
    bf16 = jnp.bfloat16
    dma = pltpu.SemaphoreType.DMA
    vmem = pl.BlockSpec(memory_space=pltpu.VMEM)
    return tuple(
        pl.pallas_call(
            kernel,
            out_shape=(jax.ShapeDtypeStruct((SUB, D), bf16), jax.ShapeDtypeStruct((D, F), bf16)),
            in_specs=[pl.BlockSpec(memory_space=pltpu.HBM)] * 4,
            out_specs=(vmem, vmem),
            scratch_shapes=[
                pltpu.VMEM((HALF, F), bf16),
                pltpu.VMEM((HALF, F), bf16),
                pltpu.VMEM((D, F), bf16),
                pltpu.VMEM((NZ, BLOCK, D), bf16),
                pltpu.VMEM((NY, BLOCK, F), bf16),
                pltpu.VMEM((8, BLOCK, D), bf16),
                pltpu.VMEM((8, 2, SUB, DH), bf16),
                pltpu.VMEM((8, 2, SUB, D), bf16),
                pltpu.VMEM((8, 2, SUB, DH), bf16),
                pltpu.VMEM((NZ, SUB, D), bf16),
                pltpu.VMEM((2, SUB, D), bf16),
                pltpu.VMEM((2, SUB, DH), bf16),
                pltpu.VMEM((2, SUB, D), bf16),
                pltpu.VMEM((4, SUB, D), bf16),
                pltpu.VMEM((D, F), jnp.float32),
                dma((4,)), dma((2, 2)), dma((2, 4, 2)), dma((2, 4, 2)), dma((8, 2)), dma((8, 2)),
                dma((7,)), dma((7,)), dma((2,)), dma((2,)), dma((2, 4)), dma((2, 10)), dma((2, 13)),
                dma((8, 2)), dma((8, 2)), dma((8, 2)), dma((8, 2)), dma((8, 2)), dma((8, 2)),
                dma((2, 3)), dma((4,)), dma((2,)), dma((2,)), dma((2,)),
            ],
            compiler_params=pltpu.CompilerParams(
                collective_id=0, has_side_effects=True, vmem_limit_bytes=48 * 2**20
            ),
            cost_estimate=pl.CostEstimate(flops=4 * 2048 * D * F, bytes_accessed=6 * 2**20, transcendentals=HALF * F),
            name="up_gelu_backward",
        )(*(pltpu.with_memory_space_constraint(a, pltpu.HBM) for a in (inputs, pre_act, grad_act, up_weight)))
    )


def solution(mesh):
    placed = (P("col", "row"), P("row", "col"), P("row", "col"), P("row", "col"))
    return jax.shard_map(
        on_device,
        mesh=mesh,
        in_specs=placed,
        out_specs=(P("col", "row"), P("row", "col")),
        check_vma=False,
    )
```

```python
import functools
import math

import jax
import jax.numpy as jnp
from jax import lax
from jax.experimental import pallas as pl
from jax.experimental.pallas import tpu as pltpu
from jax.sharding import PartitionSpec as P

MESH = pl.DeviceIdType.MESH
curve = math.sqrt(2.0 / math.pi)
cubic = 0.044715

NY, NZ, NX = 8, 8, 4
SUB = 64
BLOCK = 256
HALF = 128
D = 768
F = 768
DH = D // 2


def gelu_back(pre_act, grad_act):
    h = pre_act.astype(jnp.float32)
    t = jnp.tanh(curve * (h + cubic * h * h * h))
    slope = 0.5 * (1.0 + t) + 0.5 * h * (1.0 - t * t) * curve * (1.0 + 3.0 * cubic * h * h)
    return (grad_act.astype(jnp.float32) * slope).astype(jnp.bfloat16)


ORDER = (
    (0, 1, 7, 2, 3, 4, 5, 6),
    (1, 0, 2, 3, 4, 5, 6, 7),
    (2, 1, 3, 0, 4, 5, 6, 7),
    (3, 2, 4, 1, 0, 5, 6, 7),
    (4, 3, 5, 2, 1, 0, 6, 7),
    (5, 4, 6, 3, 0, 1, 2, 7),
    (6, 5, 7, 0, 1, 2, 3, 4),
    (7, 0, 6, 1, 2, 3, 4, 5),
)
MATMUL_AT = (1, 3, 4, 5, 7, 9, 10, 11)
HALF_AT = (3, 5, 6, 7, 9, 11, 12, 13)
FULL_AT = (6, 8, 9, 11, 13, 14, 15, 16)
SHARD_AT = (1, 3, 4, 5, 6, 7, 8, 10, 11, 13, 15)
MID_AT = (9, 11, 12, 14, 16, 17, 18, 19)


def turn(e, steps):
    index, due = 0, e == steps[0]
    for n in range(1, len(steps)):
        index = jnp.where(e >= steps[n], n, index)
        due = due | (e == steps[n])
    return index, due


def offset(s):
    return jnp.where((s & 1) == 1, -lax.shift_right_logical(s + 1, 1), lax.shift_right_logical(s, 1))


def kernel(
    inp, pre_hbm, grad_hbm, w_hbm, ig, wg,
    pre, grad, w, i_all, g_all, part, half_in, full_in, full_out, reduced, mid_full, mid_half, mid_out, z_in, acc,
    load, y_own, y_send, y_recv, c_send, c_recv, ix_send, ix_recv, ix_half_send, ix_half_recv, i3_send, i3_recv, iz_own, iz_send, iz_recv,
    h_send, h_recv, g_send, g_recv, f_send, f_recv, z_send, z_recv, half_send, mid_recv, mid_half_recv,
):
    row, col = lax.axis_index("row"), lax.axis_index("col")
    y, k, z, x = row // 2, row & 1, col // NX, col & (NX - 1)

    def at(dy=0, flip=False, dz=0, dx=0):
        core = 1 - k if flip else k
        return (((y + dy) & (NY - 1)) * 2 + core, ((z + dz) & (NZ - 1)) * NX + ((x + dx) & (NX - 1)))

    def send(src, dst, ssem, rsem, device):
        pltpu.make_async_remote_copy(
            src_ref=src, dst_ref=dst, send_sem=ssem, recv_sem=rsem, device_id=device, device_id_type=MESH
        ).start()

    def wait(ref, sem):
        pltpu.make_async_copy(ref, ref, sem).wait()

    def sub(j):
        return pl.ds(pl.multiple_of(((x + j) & (NX - 1)) * SUB, SUB), SUB)

    def chunk(ch):
        return pl.ds(pl.multiple_of(k * HALF + ch * SUB, SUB), SUB)

    def other_chunk(ch):
        return pl.ds(pl.multiple_of((1 - k) * HALF + ch * SUB, SUB), SUB)

    places = pick(y, [sum(t << (3 * s) for s, t in enumerate(order)) for order in ORDER])

    def block_of(s):
        return lax.shift_right_logical(places, 3 * s) & 7

    own = i_all.at[z, sub(0)]
    pre_load = pltpu.make_async_copy(pre_hbm, pre, load.at[0])
    grad_load = pltpu.make_async_copy(grad_hbm, grad, load.at[1])
    inp_load = pltpu.make_async_copy(inp, own, load.at[2])
    w_load = pltpu.make_async_copy(w_hbm, w, load.at[3])
    for copy in (pre_load, grad_load, inp_load, w_load):
        copy.start()

    barrier = pltpu.get_barrier_semaphore()
    peers = [at(dz=d) for d in (1, -1, 2, -2)] + [at(dx=d) for d in (1, 2, 3)]
    peers += [at(dy=1), at(dy=-1), at(flip=True)]
    for peer in peers:
        pl.semaphore_signal(barrier, inc=1, device_id=peer, device_id_type=MESH)
    pre_load.wait()
    grad_load.wait()
    for ch in range(2):

        @pl.loop(0, SUB // 16)
        def _(r):
            src = pl.ds(pl.multiple_of(ch * SUB + r * 16, 16), 16)
            dst = pl.ds(pl.multiple_of(k * HALF + ch * SUB + r * 16, 16), 16)
            g_all[y, dst, :] = gelu_back(pre[src, :], grad[src, :])

        if ch == 0:
            pl.semaphore_wait(barrier, len(peers))
        mine = g_all.at[y, chunk(ch)]
        send(mine, mine, y_own.at[0, ch], y_recv.at[0, 0, ch], at(dy=1))
        send(mine, mine, y_own.at[1, ch], y_recv.at[1, 0, ch], at(dy=-1))
        send(mine, mine, c_send.at[0, ch], c_recv.at[0, ch], at(flip=True))
        if ch == 0:
            inp_load.wait()
            send(own, own, iz_own.at[0, 0], iz_recv.at[0, 0], at(dz=1))
            send(own, own, iz_own.at[1, 0], iz_recv.at[1, 0], at(dz=-1))
            for j in (1, 3):
                send(own, own, ix_send.at[j], ix_recv.at[NX - j], at(dx=j))

    shard = i_all.at[0, pl.ds(0, SUB)]
    half_shard = i_all.at[0, pl.ds(0, SUB // 2)]
    acc[...] = jnp.zeros_like(acc)
    w_load.wait()

    @pl.loop(1, 21)
    def _(e):
        s, due1 = turn(e, MATMUL_AT)

        @pl.when(due1)
        def _():
            t = block_of(s)
            ahead = (t - y) & (NY - 1)
            arrival = jnp.where(ahead <= 3, 2 * ahead, 2 * (NY - ahead) - 1)
            for ch in range(2):
                wait(g_all.at[t, other_chunk(ch)], c_recv.at[arrival, ch])
            part[s] = lax.dot_general(
                g_all[t], w[...], (((1,), (1,)), ((), ())), preferred_element_type=jnp.float32
            ).astype(jnp.bfloat16)
            send(part.at[s, sub(2), pl.ds(0, DH)], half_in.at[s, 0], h_send.at[s, 0], h_recv.at[s, 0], at(dx=1))
            send(part.at[s, sub(2), pl.ds(DH, DH)], half_in.at[s, 1], h_send.at[s, 1], h_recv.at[s, 1], at(dx=-1))
            for way in range(2):
                hi = pl.ds((1 - way) * DH, DH)
                send(
                    part.at[s, sub(1 - 2 * way), hi], full_in.at[s, way, :, hi],
                    g_send.at[s, way], g_recv.at[s, way], at(dx=1 - 2 * way),
                )

        @pl.when(e <= 7)
        def _():
            hop = lax.shift_right_logical(e + 1, 1)
            for way in range(2):
                ch = jnp.where(e == 7, way, (e - 1) & 1)
                s = jnp.minimum(2 * hop - 1 + way, 7)
                block = g_all.at[(y - hop * (1 - 2 * way)) & (NY - 1), chunk(ch)]
                wait(block, y_recv.at[way, hop - 1, ch])
                onward = (hop <= 2) | ((hop == 3) & (ch == way))

                @pl.when(onward)
                def _():
                    send(block, block, y_send.at[way, hop, ch], y_recv.at[way, hop, ch], at(dy=1 - 2 * way))

                send(block, block, c_send.at[s, ch], c_recv.at[s, ch], at(flip=True))

        b, due = turn(e, HALF_AT)

        @pl.when(due)
        def _():
            for way in range(2):
                wait(half_in.at[b, way], h_recv.at[b, way])
                dest = sub(1 - 2 * way)
                lo = pl.ds(way * DH, DH)
                full_out[b, way] = (
                    part[b, dest, lo].astype(jnp.float32) + half_in[b, way].astype(jnp.float32)
                ).astype(jnp.bfloat16)
                send(
                    full_out.at[b, way], full_in.at[b, way, :, lo],
                    f_send.at[b, way], f_recv.at[b, way], at(dx=1 - 2 * way),
                )

        b3, due3 = turn(e, FULL_AT)

        @pl.when(due3)
        def _():
            owner = block_of(b3)
            ahead = (owner - z) & (NZ - 1)
            for way in range(2):
                wait(full_in.at[b3, way, :, pl.ds((1 - way) * DH, DH)], g_recv.at[b3, way])
                wait(full_in.at[b3, way, :, pl.ds(way * DH, DH)], f_recv.at[b3, way])
            total = part[b3, sub(0), :].astype(jnp.float32)
            total = total + full_in[b3, 0].astype(jnp.float32) + full_in[b3, 1].astype(jnp.float32)
            reduced[owner] = total.astype(jnp.bfloat16)
            whole = reduced.at[owner]
            for way in range(2):

                @pl.when(ahead == (1, 7)[way])
                def _():
                    send(whole, z_in.at[way], z_send.at[way, 0], z_recv.at[way], at(dz=1 - 2 * way))

                @pl.when(ahead == (3, 5)[way])
                def _():
                    send(whole, mid_full.at[way], z_send.at[way, 1], mid_recv.at[way], at(dz=1 - 2 * way))

                @pl.when(ahead == 4)
                def _():
                    half = reduced.at[owner, :, pl.ds(way * DH, DH)]
                    send(half, mid_half.at[way], half_send.at[way], mid_half_recv.at[way], at(dz=2 - 4 * way))

        b4, due4 = turn(e, MID_AT)

        @pl.when(due4)
        def _():
            owner = block_of(b4)
            ahead = (owner - z) & (NZ - 1)
            for way in range(2):

                @pl.when(ahead == (2, 6)[way])
                def _():
                    wait(mid_full.at[way], mid_recv.at[way])
                    wait(mid_half.at[way], mid_half_recv.at[way])
                    lo, hi = pl.ds(way * DH, DH), pl.ds((1 - way) * DH, DH)
                    mid_out[way, :, lo] = (
                        reduced[owner, :, lo].astype(jnp.float32)
                        + mid_full[way, :, lo].astype(jnp.float32)
                        + mid_half[way].astype(jnp.float32)
                    ).astype(jnp.bfloat16)
                    mid_out[way, :, hi] = (
                        reduced[owner, :, hi].astype(jnp.float32) + mid_full[way, :, hi].astype(jnp.float32)
                    ).astype(jnp.bfloat16)
                    send(mid_out.at[way], z_in.at[2 + way], z_send.at[way, 2], z_recv.at[2 + way], at(dz=2 - 4 * way))

        def quarter(j, way):
            return i_all.at[z, pl.ds(pl.multiple_of(((x + j) & (NX - 1)) * SUB + way * (SUB // 2), SUB // 2), SUB // 2)]

        def from_x(j):
            block = i_all.at[z, sub(j)]
            if j == 2:
                for way in range(2):
                    wait(quarter(2, way), ix_half_recv.at[way])
            else:
                wait(block, ix_recv.at[j])
                way = 0 if j == 3 else 1
                part_of = quarter(j, way)
                send(part_of, part_of, ix_half_send.at[way], ix_half_recv.at[way], at(dx=1 - 2 * way))
            send(block, block, iz_own.at[0, j], iz_recv.at[0, j], at(dz=1))
            send(block, block, iz_own.at[1, j], iz_recv.at[1, j], at(dz=-1))

        @pl.when(e == 16)
        def _():
            for j in (1, 3):
                wait(shard, ix_send.at[j])
            for way in range(2):
                wait(half_shard, ix_half_send.at[way])
                for j in range(4):
                    wait(shard, iz_own.at[way, j])
                for u in (0, 1, 2, 4, 6, 9):
                    wait(shard, iz_send.at[way, u])
                wait(half_shard, iz_send.at[way, 3])
                for ch in range(2):
                    wait(shard, y_own.at[way, ch])
                    for hop in (1, 2):
                        wait(shard, y_send.at[way, hop, ch])
                wait(shard, y_send.at[way, 3, way])
            for s in range(8):
                for ch in range(2):
                    wait(shard, c_send.at[s, ch])
                for way in range(2):
                    wait(half_in.at[0, 0], h_send.at[s, way])
                    wait(half_in.at[0, 0], g_send.at[s, way])
                    wait(half_in.at[0, 0], f_send.at[s, way])

        u, due5 = turn(e, SHARD_AT)

        @pl.when(due5)
        def _():
            zhop = pick(u, (1, 2, 1, 3, 1, 4, 1, 2, 2, 2, 3))
            j = pick(u, (0, 0, 1, 0, 3, 0, 2, 1, 3, 2, 2))
            for way in range(2):
                owner = (z - zhop * (1 - 2 * way)) & (NZ - 1)
                block = i_all.at[owner, sub(j)]
                half = i_all.at[owner, pl.ds(pl.multiple_of(x * SUB + way * (SUB // 2), SUB // 2), SUB // 2)]

                @pl.when(zhop <= 3)
                def _():
                    wait(block, iz_recv.at[way, zhop * 4 - 4 + j])

                @pl.when(zhop == 4)
                def _():
                    wait(half, iz_recv.at[way, 12])

                @pl.when((zhop == 1) | ((zhop == 2) & ((j & 1) == 0)))
                def _():
                    send(block, block, iz_send.at[way, u], iz_recv.at[way, zhop * 4 + j], at(dz=1 - 2 * way))

                @pl.when((zhop == 3) & (j == 0))
                def _():
                    send(half, half, iz_send.at[way, u], iz_recv.at[way, 12], at(dz=1 - 2 * way))

        for step, j in ((1, 1), (2, 3), (4, 2)):

            @pl.when(e == step)
            def _():
                from_x(j)

        @pl.when(e == 13)
        def _():
            block = i_all.at[(z + 4) & (NZ - 1), sub(0)]
            for j in (1, 3, 2):
                send(block, block, ix_send.at[3 + j], ix_recv.at[3 + NX - j], at(dx=j))
            for way in range(2):
                block = i_all.at[(z - 3 + 6 * way) & (NZ - 1), sub(0)]
                for n, j in enumerate((1, 3)):
                    send(block, block, i3_send.at[way, n], i3_recv.at[way, 1 - n], at(dx=j))

        @pl.when(e == 18)
        def _():
            for j in (1, 3, 2):
                wait(i_all.at[(z + 4) & (NZ - 1), sub(j)], ix_recv.at[3 + j])

        for way in range(2):

            @pl.when(e == 19 + way)
            def _():
                for n, j in enumerate((1, 3)):
                    wait(i_all.at[(z - 3 + 6 * way) & (NZ - 1), sub(j)], i3_recv.at[way, n])

        def term(q, cols):
            b = (z + offset(q)) & (NZ - 1)
            return lax.dot_general(
                i_all[b, :, cols], g_all[b], (((0,), (0,)), ((), ())), preferred_element_type=jnp.float32
            )

        @pl.when(((e >= 11) & (e <= 15)) | (e == 18) | (e == 19))
        def _():
            q = jnp.where(e <= 15, e - 11, jnp.where(e == 18, 7, e - 14))
            for n in range(3):
                cols = pl.ds(n * 256, 256)
                acc[cols, :] += term(q, cols)

        @pl.when(e == 20)
        def _():
            for n in range(3):
                cols = pl.ds(n * 256, 256)
                wg[cols, :] = (acc[cols, :] + term(jnp.int32(6), cols)).astype(jnp.bfloat16)

    for j in (4, 5, 6):
        wait(shard, ix_send.at[j])
    for way in range(2):
        for n in range(2):
            wait(shard, i3_send.at[way, n])
    for n in range(4):
        wait(z_in.at[n], z_recv.at[n])

    @pl.loop(0, SUB // 16)
    def _(r):
        rows = pl.ds(pl.multiple_of(r * 16, 16), 16)
        total = reduced[z, rows, :].astype(jnp.float32)
        for n in range(4):
            total = total + z_in[n, rows, :].astype(jnp.float32)
        ig[rows, :] = total.astype(jnp.bfloat16)

    for way in range(2):
        for n in range(3):
            wait(shard, z_send.at[way, n])
        wait(mid_half.at[way], half_send.at[way])


def pick(n, table):
    value = table[-1]
    for m in range(len(table) - 1):
        value = jnp.where(n == m, table[m], value)
    return value


def on_device(inputs, pre_act, grad_act, up_weight):
    bf16 = jnp.bfloat16
    dma = pltpu.SemaphoreType.DMA
    vmem = pl.BlockSpec(memory_space=pltpu.VMEM)
    return tuple(
        pl.pallas_call(
            kernel,
            out_shape=(jax.ShapeDtypeStruct((SUB, D), bf16), jax.ShapeDtypeStruct((D, F), bf16)),
            in_specs=[pl.BlockSpec(memory_space=pltpu.HBM)] * 4,
            out_specs=(vmem, vmem),
            scratch_shapes=[
                pltpu.VMEM((HALF, F), bf16),
                pltpu.VMEM((HALF, F), bf16),
                pltpu.VMEM((D, F), bf16),
                pltpu.VMEM((NZ, BLOCK, D), bf16),
                pltpu.VMEM((NY, BLOCK, F), bf16),
                pltpu.VMEM((8, BLOCK, D), bf16),
                pltpu.VMEM((8, 2, SUB, DH), bf16),
                pltpu.VMEM((8, 2, SUB, D), bf16),
                pltpu.VMEM((8, 2, SUB, DH), bf16),
                pltpu.VMEM((NZ, SUB, D), bf16),
                pltpu.VMEM((2, SUB, D), bf16),
                pltpu.VMEM((2, SUB, DH), bf16),
                pltpu.VMEM((2, SUB, D), bf16),
                pltpu.VMEM((4, SUB, D), bf16),
                pltpu.VMEM((D, F), jnp.float32),
                dma((4,)), dma((2, 2)), dma((2, 4, 2)), dma((2, 4, 2)), dma((8, 2)), dma((8, 2)),
                dma((7,)), dma((7,)), dma((2,)), dma((2,)), dma((2, 2)), dma((2, 2)), dma((2, 4)), dma((2, 10)), dma((2, 13)),
                dma((8, 2)), dma((8, 2)), dma((8, 2)), dma((8, 2)), dma((8, 2)), dma((8, 2)),
                dma((2, 3)), dma((4,)), dma((2,)), dma((2,)), dma((2,)),
            ],
            compiler_params=pltpu.CompilerParams(
                collective_id=0, has_side_effects=True, vmem_limit_bytes=48 * 2**20
            ),
            cost_estimate=pl.CostEstimate(flops=4 * 2048 * D * F, bytes_accessed=6 * 2**20, transcendentals=HALF * F),
            name="up_gelu_backward",
        )(*(pltpu.with_memory_space_constraint(a, pltpu.HBM) for a in (inputs, pre_act, grad_act, up_weight)))
    )


def solution(mesh):
    placed = (P("col", "row"), P("row", "col"), P("row", "col"), P("row", "col"))
    return jax.shard_map(
        on_device,
        mesh=mesh,
        in_specs=placed,
        out_specs=(P("col", "row"), P("row", "col")),
        check_vma=False,
    )
```
